32 devices in a mesh: dp: 8 (over y, x, core), node: 4 (over z).
Axes of the slice: x: 2, y: 2, z: 4, core: 2. Of those that a mesh axis runs over, the one named last changes fastest.
Arguments:
- tokens: bfloat16 [16384, 8192], P(('dp', 'node')), may hold values from -6 to 6
- weight_codes: bfloat16 [8192, 1024], P('node'), may hold values from -4 to 4
- block_scales: float32 [64, 8], P('node'), may hold values from 0.0055242716 to 0.022097087
- value_grad: bfloat16 [16384, 1024], P(('dp', 'node')), may hold values from -6 to 6
Outputs:
- values: bfloat16 [16384, 1024], P(('dp', 'node'))
- input_grad: bfloat16 [16384, 8192], P(('dp', 'node'))
- weight_grad: float32 [8192, 1024], P(('dp', 'node'))
The draws below stay inside these ranges and needn't reach their ends.
All inputs are finite; a program needn't handle non-finite values.
Results may differ from the reference program's by a relative error of at most 0.0055.
Values may be sent and summed in bfloat16 or wider, within the bound.
A program may use at most 192 MiB of HBM per device.

```python
import math
import jax
import jax.numpy as jnp
from jax import lax

D = 8192
KVW = 1024
BLK = 128
TOK_DEV = 512
TOKENS = 16384


def raised(entries, key, source, target, parts, factor):
    def block_of(dim):
        return (jnp.arange(entries.shape[dim]) // (entries.shape[dim] // parts)).reshape((-1,) + (1,) * (entries.ndim - 1 - dim))

    first = jax.random.permutation(key, parts)[block_of(target)]
    other_side = (block_of(target) + parts // 2) % parts
    return jnp.where((block_of(source) == first) | (block_of(source) == other_side), factor * entries, entries)


def block_levels(rng, dims, shards, low, high):
    loudness = 1.0
    for dim, shards_of in shards:
        steps = jax.random.uniform(jax.random.fold_in(jax.random.fold_in(rng, 6), dim), (shards_of,), jnp.float32, low / len(shards), high / len(shards))
        loudness = loudness * jnp.repeat(jnp.exp(steps), dims[dim] // shards_of).reshape((-1,) + (1,) * (len(dims) - 1 - dim))
    return loudness


def bell_draw(own_key, shape, spread, most, cuts=(), held_as=jnp.bfloat16):
    array = spread * jax.random.normal(own_key, shape, jnp.float32)
    if cuts:
        array = array * block_levels(own_key, shape, cuts, -0.22, 0.18)
    return jnp.clip(array, -most, most).astype(held_as)


def gaussian_with(own_key, dims, deviation, reach, shards, heavy, kind=jnp.bfloat16):
    array = deviation * jax.random.normal(own_key, dims, jnp.float32)
    if shards:
        array = array * block_levels(own_key, dims, shards, -0.22, 0.18)
    return jnp.clip(raised(array, jax.random.fold_in(own_key, 3), *heavy), -reach, reach).astype(kind)


def setup_inputs(seed: int = 0) -> dict:
    streams_of = jax.random.split(jax.random.key(seed), 5)
    return {
        "tokens": gaussian_with(streams_of[0], (TOKENS, D), 1.0, 6.0, ((0, 32),), (0, 1, 32, 2.75)),
        "weight_codes": bell_draw(streams_of[1], (D, KVW), 1.0, 4.0, ((0, 4),)),
        "block_scales": jnp.clip(jnp.exp(math.log(0.022097087) - 1.3862944 * jax.random.uniform(streams_of[2], (D // BLK, KVW // BLK), jnp.float32) ** block_levels(streams_of[2], (D // BLK, KVW // BLK), ((0, 4),), -0.2, 0.2)), 0.0055242716, 0.022097087),
        "value_grad": bell_draw(streams_of[3], (TOKENS, KVW), 1.0, 6.0, ((0, 32),)),
    }


def reference(tokens, weight_codes, block_scales, value_grad):
    row_blocks = D // BLK
    col_blocks = KVW // BLK
    scaled = weight_codes.astype(jnp.float32).reshape(row_blocks, BLK, col_blocks, BLK) * block_scales[:, None, :, None]
    weight = scaled.reshape(D, KVW).astype(jnp.bfloat16)
    values = jnp.dot(tokens, weight, preferred_element_type=jnp.float32).astype(jnp.bfloat16)
    input_grad = jnp.dot(value_grad, weight.T, preferred_element_type=jnp.float32).astype(jnp.bfloat16)
    loss_scale = TOKENS ** -0.5

    def add_group(running, block_pair):
        token_block, grad_block = block_pair
        product = lax.dot_general(token_block, grad_block, (((0,), (0,)), ((), ())), preferred_element_type=jnp.float32)
        grad_term = (product * loss_scale).astype(jnp.bfloat16)
        return running + grad_term.astype(jnp.float32), None

    start = jnp.zeros((D, KVW), jnp.float32)
    groups = TOKENS // TOK_DEV
    weight_grad, _ = lax.scan(add_group, start, (tokens.reshape(groups, TOK_DEV, D), value_grad.reshape(groups, TOK_DEV, KVW)))
    return values, input_grad, weight_grad
```

```python
import jax
import jax.numpy as jnp
from jax import lax
from jax.sharding import PartitionSpec as P


def dequantized(weight_codes, block_scales):
    row_count, col_count = weight_codes.shape
    row_blocks, col_blocks = block_scales.shape
    scaled = (
        weight_codes.astype(jnp.float32).reshape(
            row_blocks, row_count // row_blocks, col_blocks, col_count // col_blocks
        )
        * block_scales[:, None, :, None]
    )
    return scaled.reshape(row_count, col_count).astype(jnp.bfloat16)


def scattered_sum(term, data_count, node_count, chunk_count):
    data_index = lax.axis_index("dp")
    node_index = lax.axis_index("node")
    bits = data_count.bit_length() - 1
    width = term.shape[1] // chunk_count
    rows = term.shape[0] // (data_count * node_count)
    sums = []
    for chunk in range(chunk_count):
        block = term[:, chunk * width:(chunk + 1) * width]
        order = list(range(1, bits))
        turn = chunk % len(order) if order else 0
        order = list(range(min(bits, 1))) + order[turn:] + order[:turn]
        left = list(range(bits))
        for bit in order:
            stride = 1 << bit
            pairs = [(i, i ^ stride) for i in range(data_count)]
            mine = (data_index // stride) % 2
            inner = rows * node_count << sum(1 for other in left if other < bit)
            view = block.reshape(-1, 2, inner, width)
            going = lax.dynamic_index_in_dim(view, 1 - mine, 1, keepdims=False)
            kept = lax.dynamic_index_in_dim(view, mine, 1, keepdims=False)
            came = lax.ppermute(going, "dp", pairs)
            block = (kept.astype(jnp.float32) + came.astype(jnp.float32)).astype(jnp.bfloat16)
            left.remove(bit)
        view = block.reshape(node_count, rows, width)
        total = lax.dynamic_index_in_dim(view, node_index, 0, keepdims=False).astype(jnp.float32)
        for shift in range(1, node_count):
            target = (node_index + shift) % node_count
            going = lax.dynamic_index_in_dim(view, target, 0, keepdims=False)
            pairs = [(i, (i + shift) % node_count) for i in range(node_count)]
            total = total + lax.ppermute(going, "node", pairs).astype(jnp.float32)
        sums.append(total)
    return jnp.concatenate(sums, axis=1)


def whole_weight(local_weight, data_count, node_count, part_count):
    data_index = lax.axis_index("dp")
    node_index = lax.axis_index("node")
    bits = data_count.bit_length() - 1
    rows = local_weight.shape[0] // data_count
    width = local_weight.shape[1] // part_count
    piece = lax.dynamic_slice_in_dim(local_weight, data_index * rows, rows, 0)
    parts = []
    for part in range(part_count):
        own = piece[:, part * width:(part + 1) * width]
        held = jnp.zeros((node_count, rows, width), local_weight.dtype)
        held = lax.dynamic_update_index_in_dim(held, own, node_index, 0)
        for shift in range(1, node_count):
            pairs = [(i, (i + shift) % node_count) for i in range(node_count)]
            came = lax.ppermute(own, "node", pairs)
            held = lax.dynamic_update_index_in_dim(held, came, (node_index - shift) % node_count, 0)
        order = list(range(1, bits))
        turn = part % len(order) if order else 0
        order = order[turn:] + order[:turn] + list(range(min(bits, 1)))
        done = []
        block = held.reshape(node_count, 1, rows, width)
        for bit in order:
            stride = 1 << bit
            pairs = [(i, i ^ stride) for i in range(data_count)]
            mine = (data_index // stride) % 2
            came = lax.ppermute(block, "dp", pairs)
            low = sum(1 for other in done if other < bit)
            high = len(done) - low
            here = block.reshape(node_count, 1 << high, 1, (1 << low), rows, width)
            there = came.reshape(here.shape)
            first = jnp.where(mine == 0, here, there)
            second = jnp.where(mine == 0, there, here)
            block = jnp.concatenate([first, second], axis=2).reshape(node_count, -1, rows, width)
            done.append(bit)
        parts.append(block.reshape(-1, width))
    return jnp.concatenate(parts, axis=1)


def shards(tokens, weight_codes, block_scales, value_grad):
    data_count = lax.axis_size("dp")
    node_count = lax.axis_size("node")
    total_tokens = tokens.shape[0] * data_count * node_count
    local_weight = dequantized(weight_codes, block_scales)
    full_weight = whole_weight(local_weight, data_count, node_count, 2)
    product = lax.dot_general(
        tokens, value_grad, (((0,), (0,)), ((), ())), preferred_element_type=jnp.float32
    )
    grad_term = (product * total_tokens ** (-0.5)).astype(jnp.bfloat16)
    weight_grad = scattered_sum(grad_term, data_count, node_count, 2)
    values = jnp.dot(tokens, full_weight, preferred_element_type=jnp.float32).astype(jnp.bfloat16)
    input_grad = lax.dot_general(
        value_grad, full_weight, (((1,), (1,)), ((), ())), preferred_element_type=jnp.float32
    ).astype(jnp.bfloat16)
    return (values, input_grad, weight_grad)


def solution(mesh):
    in_specs = (P(("dp", "node"), None), P("node", None), P("node", None), P(("dp", "node"), None))
    out_specs = (P(("dp", "node"), None), P(("dp", "node"), None), P(("dp", "node"), None))
    return jax.shard_map(shards, mesh=mesh, in_specs=in_specs, out_specs=out_specs, check_vma=False)
```

```python
import jax
import jax.numpy as jnp
from jax import lax
from jax.sharding import Mesh, PartitionSpec as P

CHUNKS = 2


def dequantized(weight_codes, block_scales):
    row_count, col_count = weight_codes.shape
    row_blocks, col_blocks = block_scales.shape
    scaled = (
        weight_codes.astype(jnp.float32).reshape(
            row_blocks, row_count // row_blocks, col_blocks, col_count // col_blocks
        )
        * block_scales[:, None, :, None]
    )
    return scaled.reshape(row_count, col_count).astype(jnp.bfloat16)


def halved(view, mine, axis_name, pairs):
    going = lax.dynamic_index_in_dim(view, 1 - mine, 1, keepdims=False)
    kept = lax.dynamic_index_in_dim(view, mine, 1, keepdims=False)
    came = lax.ppermute(going, axis_name, pairs)
    return (kept.astype(jnp.float32) + came.astype(jnp.float32)).astype(jnp.bfloat16)


def dp_sum(block, turn):
    chip_index = lax.axis_index("chip")
    chip_count = lax.axis_size("chip")
    width = block.shape[1]
    inner = block.shape[0] // (chip_count * 2)
    block = halved(block.reshape(chip_count, 2, inner, width), lax.axis_index("core"), "core", [(0, 1), (1, 0)])
    left = list(range(chip_count.bit_length() - 1))
    turn = turn % len(left) if left else 0
    for bit in left[turn:] + left[:turn]:
        stride = 1 << bit
        pairs = [(i, i ^ stride) for i in range(chip_count)]
        lower = inner << sum(1 for other in left if other < bit)
        block = halved(block.reshape(-1, 2, lower, width), (chip_index // stride) % 2, "chip", pairs)
        left = [other for other in left if other != bit]
    return block.reshape(inner, width)


def node_sum(block):
    node_index = lax.axis_index("node")
    node_count = lax.axis_size("node")
    view = block.reshape(node_count, -1, block.shape[1])
    total = lax.dynamic_index_in_dim(view, node_index, 0, keepdims=False).astype(jnp.float32)
    for shift in range(1, node_count):
        going = lax.dynamic_index_in_dim(view, (node_index + shift) % node_count, 0, keepdims=False)
        pairs = [(i, (i + shift) % node_count) for i in range(node_count)]
        total = total + lax.ppermute(going, "node", pairs).astype(jnp.float32)
    return total


def shards(tokens, weight_codes, block_scales, value_grad):
    chip_count = lax.axis_size("chip")
    core_index = lax.axis_index("core")
    total_tokens = tokens.shape[0] * chip_count * 2 * lax.axis_size("node")
    local_weight = dequantized(weight_codes, block_scales)
    part = local_weight.shape[0] // (chip_count * 2)
    place = lax.axis_index("chip") * 2 + core_index
    piece = lax.dynamic_slice_in_dim(local_weight, place * part, part, 0)
    tokens, value_grad, piece = lax.optimization_barrier((tokens, value_grad, piece))
    full_weight = lax.all_gather(piece, ("node", "chip", "core"), axis=0, tiled=True)
    width = value_grad.shape[1] // CHUNKS
    blocks = []
    for chunk in range(CHUNKS):
        product = lax.dot_general(
            tokens,
            value_grad[:, chunk * width:(chunk + 1) * width],
            (((0,), (0,)), ((), ())),
            preferred_element_type=jnp.float32,
        )
        blocks.append(dp_sum((product * total_tokens ** (-0.5)).astype(jnp.bfloat16), chunk))
    full_weight, *blocks = lax.optimization_barrier((full_weight, *blocks))
    input_grad = lax.dot_general(
        value_grad, full_weight, (((1,), (1,)), ((), ())), preferred_element_type=jnp.float32
    ).astype(jnp.bfloat16)
    input_grad, blocks[-1] = lax.optimization_barrier((input_grad, blocks[-1]))
    values = jnp.dot(tokens, full_weight, preferred_element_type=jnp.float32).astype(jnp.bfloat16)
    weight_grad = jnp.concatenate([node_sum(block) for block in blocks], axis=1)
    return (values, input_grad, weight_grad)


def solution(mesh):
    dp, node = mesh.devices.shape
    cores = Mesh(mesh.devices.reshape(dp // 2, 2, node), ("chip", "core", "node"))
    rows = P(("chip", "core", "node"), None)
    in_specs = (rows, P("node", None), P("node", None), rows)
    return jax.shard_map(shards, mesh=cores, in_specs=in_specs, out_specs=(rows, rows, rows), check_vma=False)
```

```python
import jax
import jax.numpy as jnp
from jax import lax
from jax.sharding import Mesh, PartitionSpec as P

CHUNKS = 2


def dequantized(weight_codes, block_scales):
    row_count, col_count = weight_codes.shape
    row_blocks, col_blocks = block_scales.shape
    scaled = (
        weight_codes.astype(jnp.float32).reshape(
            row_blocks, row_count // row_blocks, col_blocks, col_count // col_blocks
        )
        * block_scales[:, None, :, None]
    )
    return scaled.reshape(row_count, col_count).astype(jnp.bfloat16)


def halved(view, mine, axis_name, pairs):
    going = lax.dynamic_index_in_dim(view, 1 - mine, 1, keepdims=False)
    kept = lax.dynamic_index_in_dim(view, mine, 1, keepdims=False)
    came = lax.ppermute(going, axis_name, pairs)
    return (kept.astype(jnp.float32) + came.astype(jnp.float32)).astype(jnp.bfloat16)


def dp_sum(block, turn):
    chip_index = lax.axis_index("chip")
    chip_count = lax.axis_size("chip")
    width = block.shape[1]
    inner = block.shape[0] // (chip_count * 2)
    block = halved(block.reshape(chip_count, 2, inner, width), lax.axis_index("core"), "core", [(0, 1), (1, 0)])
    left = list(range(chip_count.bit_length() - 1))
    turn = turn % len(left) if left else 0
    for bit in left[turn:] + left[:turn]:
        stride = 1 << bit
        pairs = [(i, i ^ stride) for i in range(chip_count)]
        lower = inner << sum(1 for other in left if other < bit)
        block = halved(block.reshape(-1, 2, lower, width), (chip_index // stride) % 2, "chip", pairs)
        left = [other for other in left if other != bit]
    return block.reshape(inner, width)


def node_sum(block):
    node_index = lax.axis_index("node")
    node_count = lax.axis_size("node")
    view = block.reshape(node_count, -1, block.shape[1])
    total = lax.dynamic_index_in_dim(view, node_index, 0, keepdims=False).astype(jnp.float32)
    for shift in range(1, node_count):
        going = lax.dynamic_index_in_dim(view, (node_index + shift) % node_count, 0, keepdims=False)
        pairs = [(i, (i + shift) % node_count) for i in range(node_count)]
        total = total + lax.ppermute(going, "node", pairs).astype(jnp.float32)
    return total


def shards(tokens, weight_codes, block_scales, value_grad):
    chip_count = lax.axis_size("chip")
    core_index = lax.axis_index("core")
    total_tokens = tokens.shape[0] * chip_count * 2 * lax.axis_size("node")
    part = weight_codes.shape[0] // (chip_count * 2)
    place = lax.axis_index("chip") * 2 + core_index
    block_rows = weight_codes.shape[0] // block_scales.shape[0]
    piece = dequantized(
        lax.dynamic_slice_in_dim(weight_codes, place * part, part, 0),
        lax.dynamic_slice_in_dim(block_scales, place * part // block_rows, max(1, part // block_rows), 0),
    )
    tokens, value_grad, piece = lax.optimization_barrier((tokens, value_grad, piece))
    full_weight = lax.all_gather(piece, ("node", "chip", "core"), axis=0, tiled=True)
    width = value_grad.shape[1] // CHUNKS
    blocks = []
    for chunk in range(CHUNKS):
        product = lax.dot_general(
            tokens,
            value_grad[:, chunk * width:(chunk + 1) * width],
            (((0,), (0,)), ((), ())),
            preferred_element_type=jnp.float32,
        )
        blocks.append(dp_sum((product * total_tokens ** (-0.5)).astype(jnp.bfloat16), chunk))
    full_weight, *blocks = lax.optimization_barrier((full_weight, *blocks))
    input_grad = lax.dot_general(
        value_grad, full_weight, (((1,), (1,)), ((), ())), preferred_element_type=jnp.float32
    ).astype(jnp.bfloat16)
    input_grad, blocks[-1] = lax.optimization_barrier((input_grad, blocks[-1]))
    values = jnp.dot(tokens, full_weight, preferred_element_type=jnp.float32).astype(jnp.bfloat16)
    weight_grad = jnp.concatenate([node_sum(block) for block in blocks], axis=1)
    return (values, input_grad, weight_grad)


def solution(mesh):
    dp, node = mesh.devices.shape
    cores = Mesh(mesh.devices.reshape(dp // 2, 2, node), ("chip", "core", "node"))
    rows = P(("chip", "core", "node"), None)
    in_specs = (rows, P("node", None), P("node", None), rows)
    return jax.shard_map(shards, mesh=cores, in_specs=in_specs, out_specs=(rows, rows, rows), check_vma=False)
```
